32 devices in a mesh: req: 8 (over z, x), tp: 4 (over y, core).
Axes of the slice: x: 2, y: 2, z: 4, core: 2. Of those that a mesh axis runs over, the one named last changes fastest.
Arguments:
- queries: bfloat16 [256, 7168], P('req', 'tp')
- new_keys: bfloat16 [256, 1024], P('req', 'tp'), may hold values from -6 to 6
- new_values: bfloat16 [256, 1024], P('req', 'tp'), may hold values from -6 to 6
- cache_keys: bfloat16 [143360, 1024], P('req', 'tp'), may hold values from -6 to 6
- cache_values: bfloat16 [143360, 1024], P('req', 'tp'), may hold values from -6 to 6
- tok_req: int32 [256], P('req'), may hold values from 0 to 16, as said below
- cache_req: int32 [143360], P('req'), may hold values from -1 to 16, as said below
- out_weight: bfloat16 [7168, 7168], P('tp', 'req'), may hold values from -0.0625 to 0.0625
- residual: bfloat16 [256, 7168], P('tp', 'req')
- norm_gain: float32 [7168], replicated, may hold values from 0.1 to 1.9
- gate_weight: bfloat16 [7168, 20480], P(None, ('req', 'tp')), may hold values from -0.0625 to 0.0625
- up_weight: bfloat16 [7168, 20480], P(None, ('req', 'tp')), may hold values from -0.0625 to 0.0625
- down_weight: bfloat16 [20480, 7168], P(('req', 'tp')), may hold values from -0.078125 to 0.078125
Outputs:
- layer_out: bfloat16 [256, 7168], P('tp', 'req')
The draws below stay inside these ranges and needn't reach their ends.
Inputs may be any that keep to these rules, and one draw needn't show every extreme that they name: `tok_req`: within a group, request 0 is the prefill request, whose tokens stand first and in order; decode requests 1, 2, ... follow with one token each. `cache_req`: -1 marks an empty slot; within a group the owned slots stand first, each request's slots together, requests in increasing order; every request of a group that has tokens owns at least one slot.
All inputs are finite; a program needn't handle non-finite values.
Results may differ from the reference program's by a relative error of at most 0.014.
Values may be sent and summed in bfloat16 or wider, within the bound.
A program may use at most 128 MiB of HBM per device.

```python
import math
import jax
import jax.numpy as jnp
from jax import lax

D = 7168
HEADS = 56
KVH = 8
HD = 128
FF = 20480
TG = 32
LONG = 8192
PREC = 1536
SHORT = 512
NGROUP = 8
TOK = 256
KB = 17920
POOL = 143360


def group_layout(key):
    key = jax.random.fold_in(key, 11)
    keys = jax.random.split(key, 6)
    prefill = (2 + jax.random.randint(keys[0], (NGROUP,), 0, 2).astype(jnp.int32)) * (TG // 4)
    half_group = jax.random.randint(keys[1], (), 0, NGROUP)
    prefill = jnp.where(jnp.arange(NGROUP) == half_group, 2 * (TG // 4), prefill).astype(jnp.int32)
    token_index = jnp.arange(TG, dtype=jnp.int32)
    tok_ids = jnp.where(token_index[None, :] < prefill[:, None], 0, token_index[None, :] - prefill[:, None] + 1).astype(jnp.int32)
    request_ids = jnp.arange(TG + 1, dtype=jnp.int32)
    decodes = TG - prefill
    long_flag = jax.random.randint(keys[2], (NGROUP,), 0, 2).astype(jnp.int32)
    prefill_len = jax.random.randint(keys[3], (NGROUP,), 1, PREC + 1).astype(jnp.int32)
    long_len = (LONG - jax.random.randint(keys[4], (NGROUP,), 0, LONG // 16)).astype(jnp.int32)
    short_len = jax.random.randint(keys[5], (NGROUP, TG + 1), 1, SHORT).astype(jnp.int32)
    decode_len = jnp.where((request_ids[None, :] == 1) & (long_flag[:, None] == 1), long_len[:, None], short_len)
    decode_len = jnp.where(request_ids[None, :] <= decodes[:, None], decode_len, 0)
    first_len = jnp.where(prefill > 0, prefill_len, 0)
    lengths = jnp.where(request_ids[None, :] == 0, first_len[:, None], decode_len).astype(jnp.int32)
    ends = jnp.cumsum(lengths, axis=1).astype(jnp.int32)
    slot_index = jnp.arange(KB, dtype=jnp.int32)
    owner = jnp.sum((slot_index[None, :, None] >= ends[:, None, :]).astype(jnp.int32), axis=2).astype(jnp.int32)
    owner = jnp.where(slot_index[None, :] < ends[:, -1:], owner, -1).astype(jnp.int32)
    return (tok_ids.reshape(TOK), owner.reshape(POOL))


def draw_tok_req(key, part):
    return group_layout(key)[0]


def draw_cache_req(key, part):
    return group_layout(key)[1]


def draw_queries(key, part):
    key = jax.random.fold_in(key, 23)
    first = jax.random.fold_in(key, 0)
    base = jax.random.normal(first, (TOK, HEADS, HD), jnp.float32)
    base = jnp.clip(base, -6.0, 6.0)
    return base.reshape(TOK, HEADS * HD).astype(jnp.bfloat16)


def draw_residual(key, part):
    key = jax.random.fold_in(key, 37)
    keys = jax.random.split(key, 3)
    column_rise = jnp.exp(math.log(3.0) * jnp.arange(D, dtype=jnp.float32) / (D - 1))
    column_scale = 0.4 * column_rise * jnp.exp(jax.random.uniform(keys[1], (D,), jnp.float32, 0.0, math.log(3.3)))
    row_scale = jnp.exp(jax.random.uniform(keys[2], (TOK, 1), jnp.float32, math.log(0.2), math.log(2.0)))
    base = jnp.clip(jax.random.normal(keys[0], (TOK, D), jnp.float32), -6.0, 6.0)
    return (base * row_scale * column_scale[None, :]).astype(jnp.bfloat16)


def with_spikes(values, key, source, target, shards_of, factor):
    def block_of(dim):
        return (jnp.arange(values.shape[dim]) // (values.shape[dim] // shards_of)).reshape((-1,) + (1,) * (values.ndim - 1 - dim))

    near = jax.random.permutation(key, shards_of)[block_of(target)]
    other_side = (block_of(target) + shards_of // 2) % shards_of
    return jnp.where((block_of(source) == near) | (block_of(source) == other_side), factor * values, values)


def block_levels(stream_key, dims, shards, low, high):
    gain = 1.0
    for axis_at, blocks in shards:
        draws = jax.random.uniform(jax.random.fold_in(jax.random.fold_in(stream_key, 6), axis_at), (blocks,), jnp.float32, low / len(shards), high / len(shards))
        gain = gain * jnp.repeat(jnp.exp(draws), dims[axis_at] // blocks).reshape((-1,) + (1,) * (len(dims) - 1 - axis_at))
    return gain


def gaussian(own_key, extent, scale, bound, pieces=(), kind=jnp.bfloat16):
    loudness = block_levels(own_key, extent, pieces, -0.22, 0.18) if pieces else 1.0
    values = jax.random.normal(own_key, extent, jnp.float32) * scale * loudness
    return jnp.minimum(jnp.maximum(values, -bound), bound).astype(kind)


def bell_draw_with(stream_key, dims, width, reach, cuts, heavy, kind=jnp.bfloat16):
    values = width * jax.random.normal(stream_key, dims, jnp.float32)
    if cuts:
        values = values * block_levels(stream_key, dims, cuts, -0.22, 0.18)
    return jnp.clip(with_spikes(values, jax.random.fold_in(stream_key, 3), *heavy), -reach, reach).astype(kind)


def setup_inputs(seed: int = 0) -> dict:
    key_list = jax.random.split(jax.random.key(seed), 14)
    queries = draw_queries(jax.random.fold_in(key_list[13], 71), 0)
    new_keys = gaussian(key_list[1], (TOK, KVH * HD), 1.0, 6.0, ((0, 8), (1, 4)))
    new_values = gaussian(key_list[2], (TOK, KVH * HD), 1.0, 6.0, ((0, 8), (1, 4)))
    cache_keys = gaussian(key_list[3], (POOL, KVH * HD), 1.0, 6.0, ((0, 8), (1, 4)))
    cache_values = gaussian(key_list[4], (POOL, KVH * HD), 1.0, 6.0, ((0, 8), (1, 4)))
    tok_req = draw_tok_req(jax.random.fold_in(key_list[13], 71), 0)
    cache_req = draw_cache_req(jax.random.fold_in(key_list[13], 71), 0)
    out_weight = gaussian(key_list[7], (HEADS * HD, D), (HEADS * HD) ** -0.5, 0.0625, ((0, 4), (1, 8)))
    residual = draw_residual(jax.random.fold_in(key_list[13], 71), 0)
    norm_gain = jnp.clip(1.0 + 0.18 * jax.random.normal(key_list[9], (D,), jnp.float32), 0.1, 1.9)
    gate_weight = gaussian(key_list[10], (D, FF), D ** -0.5, 0.0625, ((1, 32),))
    up_weight = gaussian(key_list[11], (D, FF), D ** -0.5, 0.0625, ((1, 32),))
    down_weight = bell_draw_with(key_list[12], (FF, D), FF ** -0.5, 0.078125, ((0, 32),), (0, 1, 32, 2.75))
    return {"queries": queries, "new_keys": new_keys, "new_values": new_values, "cache_keys": cache_keys, "cache_values": cache_values, "tok_req": tok_req, "cache_req": cache_req, "out_weight": out_weight, "residual": residual, "norm_gain": norm_gain, "gate_weight": gate_weight, "up_weight": up_weight, "down_weight": down_weight}


epsilon = 1e-05
masked_value = -1e+30

def group_attention(operands):
    group_queries, group_new_keys, group_new_values, group_cache_keys, group_cache_values, group_req, group_owner = operands
    group_size = HEADS // KVH
    keys_all = jnp.concatenate([group_cache_keys, group_new_keys], axis=0).astype(jnp.float32).reshape(KB + TG, KVH, HD)
    values_all = jnp.concatenate([group_cache_values, group_new_values], axis=0).astype(jnp.float32).reshape(KB + TG, KVH, HD)
    query_all = group_queries.astype(jnp.float32).reshape(TG, KVH, group_size, HD)
    scores = jnp.einsum('ikgd,jkd->kgij', query_all, keys_all) / math.sqrt(HD)
    cache_seen = group_owner[None, :] == group_req[:, None]
    positions = jnp.arange(TG, dtype=jnp.int32)
    new_seen = (group_req[None, :] == group_req[:, None]) & (positions[None, :] <= positions[:, None])
    visible = jnp.concatenate([cache_seen, new_seen], axis=1)
    masked = jnp.where(visible[None, None], scores, masked_value)
    row_max = lax.optimization_barrier(jnp.max(masked, axis=-1, keepdims=True))
    probs = jnp.where(visible[None, None], jnp.exp(masked - row_max), 0.0)
    probs = lax.optimization_barrier(probs.astype(jnp.bfloat16)).astype(jnp.float32)
    denominator = lax.optimization_barrier(jnp.sum(probs, axis=-1))
    weighted = jnp.einsum('kgij,jkd->ikgd', probs, values_all)
    result = weighted / jnp.transpose(denominator, (2, 0, 1))[..., None]
    return result.astype(jnp.bfloat16).reshape(TG, HEADS * HD)

def reference(queries, new_keys, new_values, cache_keys, cache_values, tok_req, cache_req, out_weight, residual, norm_gain, gate_weight, up_weight, down_weight):
    operands = (queries.reshape(NGROUP, TG, HEADS * HD), new_keys.reshape(NGROUP, TG, KVH * HD), new_values.reshape(NGROUP, TG, KVH * HD), cache_keys.reshape(NGROUP, KB, KVH * HD), cache_values.reshape(NGROUP, KB, KVH * HD), tok_req.reshape(NGROUP, TG), cache_req.reshape(NGROUP, KB))
    attended = lax.map(group_attention, operands).reshape(TOK, HEADS * HD)
    projected = jnp.dot(attended, out_weight, preferred_element_type=jnp.float32)
    stream = (residual.astype(jnp.float32) + projected).astype(jnp.bfloat16)
    wide = stream.astype(jnp.float32)
    mean_square = lax.optimization_barrier(jnp.mean(wide * wide, axis=1, keepdims=True))
    normed = (wide * lax.rsqrt(mean_square + epsilon) * norm_gain.astype(jnp.float32)[None, :]).astype(jnp.bfloat16)
    gate = jnp.dot(normed, gate_weight, preferred_element_type=jnp.float32)
    up = jnp.dot(normed, up_weight, preferred_element_type=jnp.float32)
    hidden = (jax.nn.silu(gate) * up).astype(jnp.bfloat16)
    mlp = jnp.dot(hidden, down_weight, preferred_element_type=jnp.float32)
    return (wide + mlp).astype(jnp.bfloat16)
```

```python
import functools
import math

import jax
import jax.numpy as jnp
from jax import lax
from jax.experimental import pallas as pl
from jax.experimental.pallas import tpu as pltpu
from jax.sharding import PartitionSpec as P

HD = 128
epsilon = 1e-05
masked_value = -1e30
key_block = 512
score_factor = math.log2(math.e) / math.sqrt(HD)
BF = jnp.bfloat16
F32 = jnp.float32


def attend_kernel(
    first_ref, count_ref, bounds_ref, q_ref, nk_ref, nv_ref, ck_ref, cv_ref, out_ref,
    kbuf, vbuf, ksem, vsem, m_ref, l_ref, acc_ref,
):
    windows = q_ref.shape[0]
    kv = q_ref.shape[2] // HD
    pool = ck_ref.shape[0]
    width = kbuf.shape[1]
    slots = kbuf.shape[0]
    ahead = slots - 1

    def copies(w, b, slot):
        start = jnp.minimum(first_ref[w] + b * width, pool - width)
        start = pl.multiple_of(start, 16)
        rows = pl.ds(start, width)
        return (
            pltpu.make_async_copy(ck_ref.at[rows], kbuf.at[slot], ksem.at[slot]),
            pltpu.make_async_copy(cv_ref.at[rows], vbuf.at[slot], vsem.at[slot]),
        )

    def advance(w, b):
        last = b + 1 >= count_ref[jnp.minimum(w, windows - 1)]
        return jnp.where(last, w + 1, w), jnp.where(last, 0, b + 1)

    def fetch(w, b, slot):
        @pl.when(w < windows)
        def _():
            for c in copies(w, b, slot):
                c.start()

    w0, b0 = jnp.int32(0), jnp.int32(0)
    for i in range(ahead):
        fetch(w0, b0, i)
        w0, b0 = advance(w0, b0)

    def col(row):
        return jnp.transpose(jnp.broadcast_to(row, (8, row.shape[1])))[:, :1]

    def scores_of(keys, w, low, high):
        s = lax.dot_general(
            keys, q_ref[w], (((1,), (1,)), ((), ())), preferred_element_type=F32
        )
        pos = lax.broadcasted_iota(jnp.int32, s.shape, 0)
        return jnp.where((pos >= low) & (pos < high), s * score_factor, masked_value)

    def weigh(p, values):
        return lax.dot_general(p, values, (((0,), (0,)), ((), ())), preferred_element_type=F32)

    def window(w, carry):
        low, high = bounds_ref[w, 0:1, :], bounds_ref[w, 1:2, :]
        s = scores_of(nk_ref[...], w, bounds_ref[w, 2:3, :], bounds_ref[w, 3:4, :])
        m = jnp.max(s, axis=0, keepdims=True)
        p = jnp.exp2(s - m).astype(BF)
        m_ref[...] = m
        l_ref[...] = jnp.sum(p.astype(F32), axis=0, keepdims=True)
        acc_ref[...] = weigh(p, nv_ref[...])

        def block(b, inner):
            item, wn, bn = inner
            slot = lax.rem(item, slots)
            fetch(wn, bn, lax.rem(item + ahead, slots))
            for c in copies(w, b, slot):
                c.wait()
            nominal = first_ref[w] + b * width
            start = jnp.minimum(nominal, pool - width)
            s = scores_of(kbuf[slot], w, jnp.maximum(low, nominal) - start, high - start)
            m_old = m_ref[...]
            m_new = jnp.maximum(m_old, jnp.max(s, axis=0, keepdims=True))
            alpha = jnp.exp2(m_old - m_new)
            p = jnp.exp2(s - m_new).astype(BF)
            m_ref[...] = m_new
            l_ref[...] = l_ref[...] * alpha + jnp.sum(p.astype(F32), axis=0, keepdims=True)
            acc_ref[...] = acc_ref[...] * col(alpha) + weigh(p, vbuf[slot])
            return (item + 1, *advance(wn, bn))

        carry = lax.fori_loop(0, count_ref[w], block, carry)
        scaled = acc_ref[...] / col(l_ref[...])
        rows = scaled.shape[0] // kv
        for h in range(kv):
            part = slice(h * rows, (h + 1) * rows)
            out_ref[w, part, :] = scaled[part, h * HD : (h + 1) * HD].astype(BF)
        return carry

    lax.fori_loop(0, windows, window, (jnp.int32(0), w0, b0))


def attend(queries, new_keys, new_values, cache_keys, cache_values, tok_req, cache_req):
    tokens = queries.shape[0]
    kv = new_keys.shape[1] // HD
    group = queries.shape[1] // (kv * HD)
    padded = (group + 7) // 8 * 8
    span = max(1, min(tokens, 128 // (padded * kv)))
    windows = tokens // span
    columns = kv * span * padded
    depth = kv * HD
    pool = cache_keys.shape[0]
    width = min(key_block, pool)

    owned = cache_req[None, :] >= 0
    low = jnp.sum((owned & (cache_req[None, :] < tok_req[:, None])).astype(jnp.int32), axis=1)
    high = jnp.sum((owned & (cache_req[None, :] <= tok_req[:, None])).astype(jnp.int32), axis=1)
    new_low = jnp.sum((tok_req[None, :] < tok_req[:, None]).astype(jnp.int32), axis=1)
    new_high = jnp.arange(1, tokens + 1, dtype=jnp.int32)
    first = jnp.min(low.reshape(windows, span), axis=1) // 16 * 16
    last = jnp.max(high.reshape(windows, span), axis=1)
    count = jnp.maximum((last - first + width - 1) // width, 1)
    bounds = jnp.stack([low, high, new_low, new_high] * 2)
    bounds = bounds.reshape(8, windows, 1, span, 1).transpose(1, 0, 2, 3, 4)
    bounds = jnp.broadcast_to(bounds, (windows, 8, kv, span, padded)).reshape(windows, 8, columns)

    q = queries.reshape(windows, span, kv, group, HD)
    q = jnp.pad(q, ((0, 0), (0, 0), (0, 0), (0, padded - group), (0, 0)))
    q = q.transpose(0, 2, 1, 3, 4).reshape(windows, kv, span * padded, 1, HD)
    q = q * jnp.eye(kv, dtype=BF)[None, :, None, :, None]
    q = q.reshape(windows, columns, depth)

    vmem = pl.BlockSpec(memory_space=pltpu.VMEM)
    smem = pl.BlockSpec(memory_space=pltpu.SMEM)
    anywhere = pl.BlockSpec(memory_space=pl.ANY)
    slots = 4
    out = pl.pallas_call(
        attend_kernel,
        out_shape=jax.ShapeDtypeStruct((windows, columns, HD), BF),
        in_specs=[smem, smem, vmem, vmem, vmem, vmem, anywhere, anywhere],
        out_specs=vmem,
        scratch_shapes=[
            pltpu.VMEM((slots, width, depth), BF),
            pltpu.VMEM((slots, width, depth), BF),
            pltpu.SemaphoreType.DMA((slots,)),
            pltpu.SemaphoreType.DMA((slots,)),
            pltpu.VMEM((1, columns), F32),
            pltpu.VMEM((1, columns), F32),
            pltpu.VMEM((columns, depth), F32),
        ],
        compiler_params=pltpu.CompilerParams(vmem_limit_bytes=24 * 2**20),
        name="attend",
    )(first, count, bounds, q, new_keys, new_values, cache_keys, cache_values)
    out = out.reshape(windows, kv, span, padded, HD)[:, :, :, :group]
    return out.transpose(0, 2, 1, 3, 4).reshape(tokens, kv * group * HD)


def per_device(
    queries, new_keys, new_values, cache_keys, cache_values, tok_req, cache_req,
    out_weight, residual, norm_gain, gate_weight, up_weight, down_weight,
):
    attended = attend(queries, new_keys, new_values, cache_keys, cache_values, tok_req, cache_req)
    partial_out = jnp.dot(
        lax.all_gather(attended, "req", axis=0, tiled=True),
        out_weight,
        preferred_element_type=F32,
    )
    mixed = lax.psum_scatter(
        partial_out.astype(BF), "tp", scatter_dimension=0, tiled=True
    ).astype(F32)
    stream = (residual.astype(F32) + mixed).astype(BF)
    whole = lax.all_gather(stream, "req", axis=1, tiled=True)
    whole = lax.all_gather(whole, "tp", axis=0, tiled=True).astype(F32)
    mean_square = jnp.mean(whole * whole, axis=1, keepdims=True)
    normed = (whole * lax.rsqrt(mean_square + epsilon) * norm_gain[None, :]).astype(BF)
    gate = jnp.dot(normed, gate_weight, preferred_element_type=F32)
    up = jnp.dot(normed, up_weight, preferred_element_type=F32)
    hidden = (jax.nn.silu(gate) * up).astype(BF)
    product = jnp.dot(hidden, down_weight, preferred_element_type=F32)
    summed = lax.psum_scatter(product, "tp", scatter_dimension=0, tiled=True)
    summed = lax.psum_scatter(summed, "req", scatter_dimension=1, tiled=True)
    return (stream.astype(F32) + summed).astype(BF)


def solution(mesh):
    in_specs = (
        P("req", "tp"),
        P("req", "tp"),
        P("req", "tp"),
        P("req", "tp"),
        P("req", "tp"),
        P("req"),
        P("req"),
        P("tp", "req"),
        P("tp", "req"),
        P(),
        P(None, ("req", "tp")),
        P(None, ("req", "tp")),
        P(("req", "tp"), None),
    )
    out_specs = P("tp", "req")
    return jax.shard_map(
        per_device, mesh=mesh, in_specs=in_specs, out_specs=out_specs, check_vma=False
    )
```

```python
import functools
import math

import jax
import jax.numpy as jnp
from jax import lax
from jax.experimental import pallas as pl
from jax.experimental.pallas import tpu as pltpu
from jax.sharding import PartitionSpec as P

HD = 128
epsilon = 1e-05
masked_value = -1e30
key_block = 512
score_factor = math.log2(math.e) / math.sqrt(HD)
BF = jnp.bfloat16
F32 = jnp.float32


def attend_kernel(
    first_ref, count_ref, bounds_ref, q_ref, nk_ref, nv_ref, ck_ref, cv_ref, out_ref,
    kbuf, vbuf, ksem, vsem, m_ref, l_ref, acc_ref,
):
    windows = q_ref.shape[0]
    kv = q_ref.shape[2] // HD
    pool = ck_ref.shape[0]
    width = kbuf.shape[1]
    slots = kbuf.shape[0]
    ahead = slots - 1

    def copies(w, b, slot):
        start = jnp.minimum(first_ref[w] + b * width, pool - width)
        start = pl.multiple_of(start, 16)
        rows = pl.ds(start, width)
        return (
            pltpu.make_async_copy(ck_ref.at[rows], kbuf.at[slot], ksem.at[slot]),
            pltpu.make_async_copy(cv_ref.at[rows], vbuf.at[slot], vsem.at[slot]),
        )

    def advance(w, b):
        last = b + 1 >= count_ref[jnp.minimum(w, windows - 1)]
        return jnp.where(last, w + 1, w), jnp.where(last, 0, b + 1)

    def fetch(w, b, slot):
        @pl.when(w < windows)
        def _():
            for c in copies(w, b, slot):
                c.start()

    w0, b0 = jnp.int32(0), jnp.int32(0)
    for i in range(ahead):
        fetch(w0, b0, i)
        w0, b0 = advance(w0, b0)

    def col(row):
        return jnp.transpose(jnp.broadcast_to(row, (8, row.shape[1])))[:, :1]

    def scores_of(keys, w, low, high):
        s = lax.dot_general(
            keys, q_ref[w], (((1,), (1,)), ((), ())), preferred_element_type=F32
        )
        pos = lax.broadcasted_iota(jnp.int32, s.shape, 0)
        return jnp.where((pos >= low) & (pos < high), s * score_factor, masked_value)

    def weigh(p, values):
        return lax.dot_general(p, values, (((0,), (0,)), ((), ())), preferred_element_type=F32)

    def window(w, carry):
        low, high = bounds_ref[w, 0:1, :], bounds_ref[w, 1:2, :]
        s = scores_of(nk_ref[...], w, bounds_ref[w, 2:3, :], bounds_ref[w, 3:4, :])
        m = jnp.max(s, axis=0, keepdims=True)
        p = jnp.exp2(s - m).astype(BF)
        m_ref[...] = m
        l_ref[...] = jnp.sum(p.astype(F32), axis=0, keepdims=True)
        acc_ref[...] = weigh(p, nv_ref[...])

        def block(b, inner):
            item, wn, bn = inner
            slot = lax.rem(item, slots)
            fetch(wn, bn, lax.rem(item + ahead, slots))
            for c in copies(w, b, slot):
                c.wait()
            nominal = first_ref[w] + b * width
            start = jnp.minimum(nominal, pool - width)
            s = scores_of(kbuf[slot], w, jnp.maximum(low, nominal) - start, high - start)
            m_old = m_ref[...]
            m_new = jnp.maximum(m_old, jnp.max(s, axis=0, keepdims=True))
            alpha = jnp.exp2(m_old - m_new)
            p = jnp.exp2(s - m_new).astype(BF)
            m_ref[...] = m_new
            l_ref[...] = l_ref[...] * alpha + jnp.sum(p.astype(F32), axis=0, keepdims=True)
            acc_ref[...] = acc_ref[...] * col(alpha) + weigh(p, vbuf[slot])
            return (item + 1, *advance(wn, bn))

        carry = lax.fori_loop(0, count_ref[w], block, carry)
        scaled = acc_ref[...] / col(l_ref[...])
        rows = scaled.shape[0] // kv
        for h in range(kv):
            part = slice(h * rows, (h + 1) * rows)
            out_ref[w, part, :] = scaled[part, h * HD : (h + 1) * HD].astype(BF)
        return carry

    lax.fori_loop(0, windows, window, (jnp.int32(0), w0, b0))


def attend(queries, new_keys, new_values, cache_keys, cache_values, tok_req, cache_req):
    tokens = queries.shape[0]
    kv = new_keys.shape[1] // HD
    group = queries.shape[1] // (kv * HD)
    padded = (group + 7) // 8 * 8
    span = max(1, min(tokens, 128 // (padded * kv)))
    windows = tokens // span
    columns = kv * span * padded
    depth = kv * HD
    pool = cache_keys.shape[0]
    width = min(key_block, pool)

    owned = cache_req[None, :] >= 0
    low = jnp.sum((owned & (cache_req[None, :] < tok_req[:, None])).astype(jnp.int32), axis=1)
    high = jnp.sum((owned & (cache_req[None, :] <= tok_req[:, None])).astype(jnp.int32), axis=1)
    new_low = jnp.sum((tok_req[None, :] < tok_req[:, None]).astype(jnp.int32), axis=1)
    new_high = jnp.arange(1, tokens + 1, dtype=jnp.int32)
    first = jnp.min(low.reshape(windows, span), axis=1) // 16 * 16
    last = jnp.max(high.reshape(windows, span), axis=1)
    count = jnp.maximum((last - first + width - 1) // width, 1)
    bounds = jnp.stack([low, high, new_low, new_high] * 2)
    bounds = bounds.reshape(8, windows, 1, span, 1).transpose(1, 0, 2, 3, 4)
    bounds = jnp.broadcast_to(bounds, (windows, 8, kv, span, padded)).reshape(windows, 8, columns)

    q = queries.reshape(windows, span, kv, group, HD)
    q = jnp.pad(q, ((0, 0), (0, 0), (0, 0), (0, padded - group), (0, 0)))
    q = q.transpose(0, 2, 1, 3, 4).reshape(windows, kv, span * padded, 1, HD)
    q = q * jnp.eye(kv, dtype=BF)[None, :, None, :, None]
    q = q.reshape(windows, columns, depth)

    vmem = pl.BlockSpec(memory_space=pltpu.VMEM)
    smem = pl.BlockSpec(memory_space=pltpu.SMEM)
    anywhere = pl.BlockSpec(memory_space=pl.ANY)
    slots = 4
    out = pl.pallas_call(
        attend_kernel,
        out_shape=jax.ShapeDtypeStruct((windows, columns, HD), BF),
        in_specs=[smem, smem, vmem, vmem, vmem, vmem, anywhere, anywhere],
        out_specs=vmem,
        scratch_shapes=[
            pltpu.VMEM((slots, width, depth), BF),
            pltpu.VMEM((slots, width, depth), BF),
            pltpu.SemaphoreType.DMA((slots,)),
            pltpu.SemaphoreType.DMA((slots,)),
            pltpu.VMEM((1, columns), F32),
            pltpu.VMEM((1, columns), F32),
            pltpu.VMEM((columns, depth), F32),
        ],
        compiler_params=pltpu.CompilerParams(vmem_limit_bytes=24 * 2**20),
        name="attend",
    )(first, count, bounds, q, new_keys, new_values, cache_keys, cache_values)
    out = out.reshape(windows, kv, span, padded, HD)[:, :, :, :group]
    return out.transpose(0, 2, 1, 3, 4).reshape(tokens, kv * group * HD)


MESH = pl.DeviceIdType.MESH
ZS = 4
shrink = 2.0**-24


def rest_kernel(
    att_ref, ow_hbm, res_ref, gain_ref, gw_hbm, uw_hbm, dw_hbm, out_ref,
    att, ow, gw, uw, dw, part, core_in, y_out, y_in, flow, gate_acc, up_acc, square_acc,
    hidden, prod, prod_core, diag_y, diag_x, from_x, from_y, from_z,
    local, send_sem, recv_sem,
):
    req, tp = lax.axis_index("req"), lax.axis_index("tp")
    z, x, y, c = req // 2, lax.rem(req, 2), tp // 2, lax.rem(tp, 2)
    columns = out_ref.shape[1]
    rows = out_ref.shape[0]
    half = rows // 2
    reqs = flow.shape[0]
    tokens = rows * flow.shape[1]
    upper, lower = pl.ds(0, half), pl.ds(half, half)

    loads = [
        pltpu.make_async_copy(ow_hbm, ow, local.at[0]),
        pltpu.make_async_copy(gw_hbm, gw, local.at[1]),
        pltpu.make_async_copy(uw_hbm, uw, local.at[2]),
    ]
    for r in range(reqs):
        part_cols = pl.ds(r * columns, columns)
        loads.append(pltpu.make_async_copy(dw_hbm.at[:, part_cols], dw.at[r], local.at[3 + r]))
    for load in loads:
        load.start()

    core_peer = (req, y * 2 + 1 - c)
    y_peer = (req, (1 - y) * 2 + c)
    x_peer = (z * 2 + 1 - x, tp)

    def z_peer(k):
        return (lax.rem(z + k, ZS) * 2 + x, tp)

    barrier = pltpu.get_barrier_semaphore()
    peers = [core_peer, y_peer, x_peer] + [z_peer(k) for k in range(1, ZS)]
    for peer in peers:
        pl.semaphore_signal(barrier, inc=1, device_id=peer, device_id_type=MESH)
    pl.semaphore_wait(barrier, len(peers))

    sent = []

    def send(src, dst, peer):
        i = len(sent)
        copy = pltpu.make_async_remote_copy(
            src_ref=src, dst_ref=dst, send_sem=send_sem.at[i], recv_sem=recv_sem.at[i],
            device_id=peer, device_id_type=MESH,
        )
        copy.start()
        sent.append(copy)
        return copy

    def behind(k):
        return lax.rem(z - k + ZS, ZS)

    along_z = [None] + [send(att_ref, att.at[req], z_peer(k)) for k in range(1, ZS)]
    across = [send(att_ref, att.at[req], x_peer)]
    att[req] = att_ref[...]
    for k in range(1, ZS):
        along_z[k].wait_recv()
        block = att.at[behind(k) * 2 + x]
        across.append(send(block, block, x_peer))
    for copy in across:
        copy.wait_recv()
    loads[0].wait()
    mixed = jnp.dot(
        att[...].reshape(tokens, att.shape[2]), ow[...], preferred_element_type=F32
    ).astype(BF).reshape(flow.shape[1], rows, columns)
    for cc in range(2):
        for yy in range(2):
            part[cc, yy] = mixed[yy * 2 + cc]
    copy = send(part.at[1 - c], core_in, core_peer)
    copy.wait_recv()
    y_out[...] = (part[c, 1 - y].astype(F32) + core_in[1 - y].astype(F32)).astype(BF)
    copy = send(y_out, y_in, y_peer)
    kept = part[c, y].astype(F32) + core_in[y].astype(F32)
    copy.wait_recv()
    stream = (res_ref[...].astype(F32) + (kept + y_in[...].astype(F32))).astype(BF)
    flow[req, tp] = stream

    def place(zz, xx, yy):
        return flow.at[zz * 2 + xx, yy * 2 + c]

    own = flow.at[req, tp]
    along_z = [None] + [send(own, own, z_peer(k)) for k in range(1, ZS)]
    to_x, to_y, turn_y, turn_x = {}, {}, {}, {}
    to_core = {k: [] for k in range(ZS)}
    gate_acc[...] = jnp.zeros_like(gate_acc)
    up_acc[...] = jnp.zeros_like(up_acc)
    square_acc[...] = jnp.zeros_like(square_acc)
    for t in range(ZS + 3):
        k = t
        if k < ZS:
            if k > 0:
                along_z[k].wait_recv()
            block = place(behind(k), x, y)
            to_x[k] = send(block, block, x_peer)
            to_y[k] = send(block, block, y_peer)
            to_core[k].append(send(block, block, core_peer))
        k = t - 1
        if 0 <= k < ZS:
            to_x[k].wait_recv()
            block = place(behind(k), 1 - x, y)
            turn_y[k] = send(block.at[upper], block.at[upper], y_peer)
            to_core[k].append(send(block, block, core_peer))
            to_y[k].wait_recv()
            block = place(behind(k), x, 1 - y)
            turn_x[k] = send(block.at[lower], block.at[lower], x_peer)
            to_core[k].append(send(block, block, core_peer))
        k = t - 2
        if 0 <= k < ZS:
            turn_y[k].wait_recv()
            turn_x[k].wait_recv()
            block = place(behind(k), 1 - x, 1 - y)
            to_core[k].append(send(block, block, core_peer))
        k = t - 3
        if 0 <= k < ZS:
            for copy in to_core[k]:
                copy.wait_recv()
            if k == 0:
                loads[1].wait()
                loads[2].wait()

            def feed(xx, unused):
                r = behind(k) * 2 + xx
                wide = flow[r].astype(F32).reshape(tokens, columns)
                square_acc[...] += jnp.sum(wide * wide, axis=1, keepdims=True)
                gained = (wide * (gain_ref[r] * shrink)).astype(BF)
                depth = pl.ds(pl.multiple_of(r * columns, columns), columns)
                gate_acc[...] += jnp.dot(gained, gw[depth, :], preferred_element_type=F32)
                up_acc[...] += jnp.dot(gained, uw[depth, :], preferred_element_type=F32)
                return unused

            lax.fori_loop(0, 2, feed, 0)

    scale = lax.rsqrt(square_acc[...] / (columns * reqs) + epsilon) * (1.0 / shrink)
    gate = gate_acc[...] * scale
    hidden[...] = (gate / (1.0 + jnp.exp(-gate)) * (up_acc[...] * scale)).astype(BF)
    for load in loads[3:]:
        load.wait()

    def ahead(k):
        return lax.rem(z + k, ZS)

    order = list(range(1, ZS)) + [0]
    to_core, turn_y, turn_x, to_x, to_y, along_z = {}, {}, {}, {}, {}, []
    for t in range(ZS + 3):
        j = t
        if j < ZS:
            to_core[j] = []
            for xx in range(2):
                r = ahead(order[j]) * 2 + xx
                term = jnp.dot(hidden[...], dw[r], preferred_element_type=F32)
                term = term.astype(BF).reshape(flow.shape[1], rows, columns)
                for cc in range(2):
                    for yy in range(2):
                        prod[r, cc, yy] = term[yy * 2 + cc]
                to_core[j].append(send(prod.at[r, 1 - c], prod_core.at[r], core_peer))
        j = t - 1
        if 0 <= j < ZS:
            for xx in range(2):
                r = ahead(order[j]) * 2 + xx
                to_core[j][xx].wait_recv()
                prod[r, c] = (prod[r, c].astype(F32) + prod_core[r].astype(F32)).astype(BF)
            block = prod.at[ahead(order[j]) * 2 + 1 - x, c, 1 - y]
            turn_y[j] = send(block.at[upper], diag_y.at[j], y_peer)
            turn_x[j] = send(block.at[lower], diag_x.at[j], x_peer)
        j = t - 2
        if 0 <= j < ZS:
            turn_y[j].wait_recv()
            block = prod.at[ahead(order[j]) * 2 + 1 - x, c, y]
            block[upper] = (block[upper].astype(F32) + diag_y[j].astype(F32)).astype(BF)
            to_x[j] = send(block, from_x.at[j], x_peer)
            turn_x[j].wait_recv()
            block = prod.at[ahead(order[j]) * 2 + x, c, 1 - y]
            block[lower] = (block[lower].astype(F32) + diag_x[j].astype(F32)).astype(BF)
            to_y[j] = send(block, from_y.at[j], y_peer)
        j = t - 3
        if 0 <= j < ZS:
            to_x[j].wait_recv()
            to_y[j].wait_recv()
            block = prod.at[ahead(order[j]) * 2 + x, c, y]
            total = block[...].astype(F32) + (from_x[j].astype(F32) + from_y[j].astype(F32))
            if order[j] > 0:
                block[...] = total.astype(BF)
                along_z.append(send(block, from_z.at[j], z_peer(order[j])))
    for j, copy in enumerate(along_z):
        copy.wait_recv()
        total = total + from_z[j].astype(F32)
    out_ref[...] = (flow[req, tp].astype(F32) + total).astype(BF)
    for copy in sent:
        copy.wait_send()


def rest(attended, out_weight, residual, norm_gain, gate_weight, up_weight, down_weight, reqs, tps):
    rows, columns = residual.shape
    tokens, depth = attended.shape
    hidden_here = gate_weight.shape[1]
    vmem = pl.BlockSpec(memory_space=pltpu.VMEM)
    anywhere = pl.BlockSpec(memory_space=pl.ANY)
    copies = 2 * ZS + 1 + (ZS - 1) + 8 * ZS + 6 * ZS + (ZS - 1)
    half = rows // 2
    return pl.pallas_call(
        rest_kernel,
        out_shape=jax.ShapeDtypeStruct((rows, columns), BF),
        in_specs=[vmem, anywhere, vmem, vmem, anywhere, anywhere, anywhere],
        out_specs=vmem,
        scratch_shapes=[
            pltpu.VMEM((reqs, tokens, depth), BF),
            pltpu.VMEM(out_weight.shape, BF),
            pltpu.VMEM(gate_weight.shape, BF),
            pltpu.VMEM(up_weight.shape, BF),
            pltpu.VMEM((reqs, hidden_here, columns), BF),
            pltpu.VMEM((2, 2, rows, columns), BF),
            pltpu.VMEM((2, rows, columns), BF),
            pltpu.VMEM((rows, columns), BF),
            pltpu.VMEM((rows, columns), BF),
            pltpu.VMEM((reqs, tps, rows, columns), BF),
            pltpu.VMEM((rows * tps, hidden_here), F32),
            pltpu.VMEM((rows * tps, hidden_here), F32),
            pltpu.VMEM((rows * tps, 1), F32),
            pltpu.VMEM((rows * tps, hidden_here), BF),
            pltpu.VMEM((reqs, 2, 2, rows, columns), BF),
            pltpu.VMEM((reqs, 2, rows, columns), BF),
            pltpu.VMEM((ZS, half, columns), BF),
            pltpu.VMEM((ZS, half, columns), BF),
            pltpu.VMEM((ZS, rows, columns), BF),
            pltpu.VMEM((ZS, rows, columns), BF),
            pltpu.VMEM((ZS - 1, rows, columns), BF),
            pltpu.SemaphoreType.DMA((3 + reqs,)),
            pltpu.SemaphoreType.DMA((copies,)),
            pltpu.SemaphoreType.DMA((copies,)),
        ],
        compiler_params=pltpu.CompilerParams(
            collective_id=0, has_side_effects=True, vmem_limit_bytes=60 * 2**20
        ),
        name="rest",
    )(
        attended, out_weight, residual, norm_gain.reshape(reqs, 1, columns),
        gate_weight, up_weight, down_weight,
    )


def per_device(
    queries, new_keys, new_values, cache_keys, cache_values, tok_req, cache_req,
    out_weight, residual, norm_gain, gate_weight, up_weight, down_weight,
):
    attended = attend(queries, new_keys, new_values, cache_keys, cache_values, tok_req, cache_req)
    reqs, tps = lax.axis_size("req"), lax.axis_size("tp")
    if reqs == 2 * ZS and tps == 4 and residual.shape[0] % 32 == 0 and residual.shape[1] % 128 == 0:
        return rest(
            attended, out_weight, residual, norm_gain, gate_weight, up_weight, down_weight, reqs, tps
        )
    partial_out = jnp.dot(
        lax.all_gather(attended, "req", axis=0, tiled=True),
        out_weight,
        preferred_element_type=F32,
    )
    mixed = lax.psum_scatter(
        partial_out.astype(BF), "tp", scatter_dimension=0, tiled=True
    ).astype(F32)
    stream = (residual.astype(F32) + mixed).astype(BF)
    whole = lax.all_gather(stream, "req", axis=1, tiled=True)
    whole = lax.all_gather(whole, "tp", axis=0, tiled=True).astype(F32)
    mean_square = jnp.mean(whole * whole, axis=1, keepdims=True)
    normed = (whole * lax.rsqrt(mean_square + epsilon) * norm_gain[None, :]).astype(BF)
    gate = jnp.dot(normed, gate_weight, preferred_element_type=F32)
    up = jnp.dot(normed, up_weight, preferred_element_type=F32)
    hidden = (jax.nn.silu(gate) * up).astype(BF)
    product = jnp.dot(hidden, down_weight, preferred_element_type=F32)
    summed = lax.psum_scatter(product, "tp", scatter_dimension=0, tiled=True)
    summed = lax.psum_scatter(summed, "req", scatter_dimension=1, tiled=True)
    return (stream.astype(F32) + summed).astype(BF)


def solution(mesh):
    in_specs = (
        P("req", "tp"),
        P("req", "tp"),
        P("req", "tp"),
        P("req", "tp"),
        P("req", "tp"),
        P("req"),
        P("req"),
        P("tp", "req"),
        P("tp", "req"),
        P(),
        P(None, ("req", "tp")),
        P(None, ("req", "tp")),
        P(("req", "tp"), None),
    )
    out_specs = P("tp", "req")
    return jax.shard_map(
        per_device, mesh=mesh, in_specs=in_specs, out_specs=out_specs, check_vma=False
    )
```

```python
import functools
import math

import jax
import jax.numpy as jnp
from jax import lax
from jax.experimental import pallas as pl
from jax.experimental.pallas import tpu as pltpu
from jax.sharding import PartitionSpec as P

HD = 128
epsilon = 1e-05
masked_value = -1e30
key_block = 1024
score_factor = math.log2(math.e) / math.sqrt(HD)
BF = jnp.bfloat16
F32 = jnp.float32


def attend_kernel(
    first_ref, count_ref, bounds_ref, q_ref, nk_ref, nv_ref, ck_ref, cv_ref, out_ref,
    kbuf, vbuf, ksem, vsem, m_ref, l_ref, acc_ref,
):
    windows = q_ref.shape[0]
    kv = q_ref.shape[2] // HD
    pool = ck_ref.shape[0]
    width = kbuf.shape[1]
    slots = kbuf.shape[0]
    ahead = slots - 1

    def copies(w, b, slot):
        start = jnp.minimum(first_ref[w] + b * width, pool - width)
        start = pl.multiple_of(start, 16)
        rows = pl.ds(start, width)
        return (
            pltpu.make_async_copy(ck_ref.at[rows], kbuf.at[slot], ksem.at[slot]),
            pltpu.make_async_copy(cv_ref.at[rows], vbuf.at[slot], vsem.at[slot]),
        )

    def advance(w, b):
        last = b + 1 >= count_ref[jnp.minimum(w, windows - 1)]
        return jnp.where(last, w + 1, w), jnp.where(last, 0, b + 1)

    def fetch(w, b, slot):
        @pl.when(w < windows)
        def _():
            for c in copies(w, b, slot):
                c.start()

    w0, b0 = jnp.int32(0), jnp.int32(0)
    for i in range(ahead):
        fetch(w0, b0, i)
        w0, b0 = advance(w0, b0)

    def scores_of(keys, w, low, high):
        s = lax.dot_general(
            q_ref[w], keys, (((1,), (1,)), ((), ())), preferred_element_type=F32
        )
        pos = lax.broadcasted_iota(jnp.int32, s.shape, 1)
        return jnp.where((pos >= low) & (pos < high), s * score_factor, masked_value)

    def weigh(p, values):
        return jnp.dot(p, values, preferred_element_type=F32)

    def window(w, carry):
        low, high = bounds_ref[w, :, 0:1], bounds_ref[w, :, 1:2]
        s = scores_of(nk_ref[...], w, bounds_ref[w, :, 2:3], bounds_ref[w, :, 3:4])
        m = jnp.max(s, axis=1, keepdims=True)
        p = jnp.exp2(s - m).astype(BF)
        m_ref[...] = m
        l_ref[...] = jnp.sum(p.astype(F32), axis=1, keepdims=True)
        acc_ref[...] = weigh(p, nv_ref[...])

        def block(b, inner):
            item, wn, bn = inner
            slot = lax.rem(item, slots)
            fetch(wn, bn, lax.rem(item + ahead, slots))
            for c in copies(w, b, slot):
                c.wait()
            nominal = first_ref[w] + b * width
            start = jnp.minimum(nominal, pool - width)
            s = scores_of(kbuf[slot], w, jnp.maximum(low, nominal) - start, high - start)
            m_old = m_ref[...]
            m_new = jnp.maximum(m_old, jnp.max(s, axis=1, keepdims=True))
            alpha = jnp.exp2(m_old - m_new)
            p = jnp.exp2(s - m_new).astype(BF)
            m_ref[...] = m_new
            l_ref[...] = l_ref[...] * alpha + jnp.sum(p.astype(F32), axis=1, keepdims=True)
            acc_ref[...] = acc_ref[...] * alpha + weigh(p, vbuf[slot])
            return (item + 1, *advance(wn, bn))

        carry = lax.fori_loop(0, count_ref[w], block, carry)
        scaled = acc_ref[...] / l_ref[...]
        rows = scaled.shape[0] // kv
        for h in range(kv):
            part = slice(h * rows, (h + 1) * rows)
            out_ref[w, part, :] = scaled[part, h * HD : (h + 1) * HD].astype(BF)
        return carry

    lax.fori_loop(0, windows, window, (jnp.int32(0), w0, b0))


def attend(queries, new_keys, new_values, cache_keys, cache_values, tok_req, cache_req):
    tokens = queries.shape[0]
    kv = new_keys.shape[1] // HD
    group = queries.shape[1] // (kv * HD)
    padded = (group + 7) // 8 * 8
    span = max(1, min(tokens, 128 // (padded * kv)))
    windows = tokens // span
    columns = kv * span * padded
    depth = kv * HD
    pool = cache_keys.shape[0]
    width = min(key_block, pool)

    owned = cache_req[None, :] >= 0
    low = jnp.sum((owned & (cache_req[None, :] < tok_req[:, None])).astype(jnp.int32), axis=1)
    high = jnp.sum((owned & (cache_req[None, :] <= tok_req[:, None])).astype(jnp.int32), axis=1)
    new_low = jnp.sum((tok_req[None, :] < tok_req[:, None]).astype(jnp.int32), axis=1)
    new_high = jnp.arange(1, tokens + 1, dtype=jnp.int32)
    first = jnp.min(low.reshape(windows, span), axis=1) // 16 * 16
    last = jnp.max(high.reshape(windows, span), axis=1)
    count = jnp.maximum((last - first + width - 1) // width, 1)
    bounds = jnp.stack([low, high, new_low, new_high], axis=1).reshape(windows, 1, span, 1, 4)
    bounds = jnp.broadcast_to(bounds, (windows, kv, span, padded, 4)).reshape(windows, columns, 4)

    q = queries.reshape(windows, span, kv, group, HD)
    q = jnp.pad(q, ((0, 0), (0, 0), (0, 0), (0, padded - group), (0, 0)))
    q = q.transpose(0, 2, 1, 3, 4).reshape(windows, kv, span * padded, 1, HD)
    q = q * jnp.eye(kv, dtype=BF)[None, :, None, :, None]
    q = q.reshape(windows, columns, depth)

    vmem = pl.BlockSpec(memory_space=pltpu.VMEM)
    smem = pl.BlockSpec(memory_space=pltpu.SMEM)
    anywhere = pl.BlockSpec(memory_space=pl.ANY)
    slots = 4
    out = pl.pallas_call(
        attend_kernel,
        out_shape=jax.ShapeDtypeStruct((windows, columns, HD), BF),
        in_specs=[smem, smem, vmem, vmem, vmem, vmem, anywhere, anywhere],
        out_specs=vmem,
        scratch_shapes=[
            pltpu.VMEM((slots, width, depth), BF),
            pltpu.VMEM((slots, width, depth), BF),
            pltpu.SemaphoreType.DMA((slots,)),
            pltpu.SemaphoreType.DMA((slots,)),
            pltpu.VMEM((columns, 1), F32),
            pltpu.VMEM((columns, 1), F32),
            pltpu.VMEM((columns, depth), F32),
        ],
        compiler_params=pltpu.CompilerParams(vmem_limit_bytes=60 * 2**20),
        name="attend",
    )(first, count, bounds, q, new_keys, new_values, cache_keys, cache_values)
    out = out.reshape(windows, kv, span, padded, HD)[:, :, :, :group]
    return out.transpose(0, 2, 1, 3, 4).reshape(tokens, kv * group * HD)


MESH = pl.DeviceIdType.MESH
ZS = 4
shrink = 2.0**-24


def rest_kernel(
    att_ref, ow_hbm, res_ref, gain_ref, gw_hbm, uw_hbm, dw_hbm, out_ref,
    att, ow, gw, uw, dw, part, core_in, y_out, y_in, flow, gate_acc, up_acc, square_acc,
    hidden, prod, prod_core, diag_y, diag_x, from_x, from_y, from_z,
    local, send_sem, recv_sem,
):
    req, tp = lax.axis_index("req"), lax.axis_index("tp")
    z, x, y, c = req // 2, lax.rem(req, 2), tp // 2, lax.rem(tp, 2)
    columns = out_ref.shape[1]
    rows = out_ref.shape[0]
    half = rows // 2
    reqs = flow.shape[0]
    tokens = rows * flow.shape[1]
    upper, lower = pl.ds(0, half), pl.ds(half, half)

    loads = [
        pltpu.make_async_copy(ow_hbm, ow, local.at[0]),
        pltpu.make_async_copy(gw_hbm, gw, local.at[1]),
        pltpu.make_async_copy(uw_hbm, uw, local.at[2]),
    ]
    for r in range(reqs):
        part_cols = pl.ds(r * columns, columns)
        loads.append(pltpu.make_async_copy(dw_hbm.at[:, part_cols], dw.at[r], local.at[3 + r]))
    for load in loads:
        load.start()

    core_peer = (req, y * 2 + 1 - c)
    y_peer = (req, (1 - y) * 2 + c)
    x_peer = (z * 2 + 1 - x, tp)

    def z_peer(k):
        return (lax.rem(z + k, ZS) * 2 + x, tp)

    barrier = pltpu.get_barrier_semaphore()
    peers = [core_peer, y_peer, x_peer] + [z_peer(k) for k in range(1, ZS)]
    for peer in peers:
        pl.semaphore_signal(barrier, inc=1, device_id=peer, device_id_type=MESH)
    pl.semaphore_wait(barrier, len(peers))

    sent = []

    def send(src, dst, peer):
        i = len(sent)
        copy = pltpu.make_async_remote_copy(
            src_ref=src, dst_ref=dst, send_sem=send_sem.at[i], recv_sem=recv_sem.at[i],
            device_id=peer, device_id_type=MESH,
        )
        copy.start()
        sent.append(copy)
        return copy

    def behind(k):
        return lax.rem(z - k + ZS, ZS)

    along_z = [None] + [send(att_ref, att.at[req], z_peer(k)) for k in range(1, ZS)]
    across = [send(att_ref, att.at[req], x_peer)]
    att[req] = att_ref[...]
    for k in range(1, ZS):
        along_z[k].wait_recv()
        block = att.at[behind(k) * 2 + x]
        across.append(send(block, block, x_peer))
    for copy in across:
        copy.wait_recv()
    loads[0].wait()
    mixed = jnp.dot(
        att[...].reshape(tokens, att.shape[2]), ow[...], preferred_element_type=F32
    ).astype(BF).reshape(flow.shape[1], rows, columns)
    for cc in range(2):
        for yy in range(2):
            part[cc, yy] = mixed[yy * 2 + cc]
    copy = send(part.at[1 - c], core_in, core_peer)
    copy.wait_recv()
    y_out[...] = (part[c, 1 - y].astype(F32) + core_in[1 - y].astype(F32)).astype(BF)
    copy = send(y_out, y_in, y_peer)
    kept = part[c, y].astype(F32) + core_in[y].astype(F32)
    copy.wait_recv()
    stream = (res_ref[...].astype(F32) + (kept + y_in[...].astype(F32))).astype(BF)
    flow[req, tp] = stream

    def place(zz, xx, yy):
        return flow.at[zz * 2 + xx, yy * 2 + c]

    own = flow.at[req, tp]
    along_z = [None] + [send(own, own, z_peer(k)) for k in range(1, ZS)]
    to_x, to_y, turn_y, turn_x = {}, {}, {}, {}
    to_core = {k: [] for k in range(ZS)}
    gate_acc[...] = jnp.zeros_like(gate_acc)
    up_acc[...] = jnp.zeros_like(up_acc)
    square_acc[...] = jnp.zeros_like(square_acc)
    for t in range(ZS + 3):
        k = t
        if k < ZS:
            if k > 0:
                along_z[k].wait_recv()
            block = place(behind(k), x, y)
            to_x[k] = send(block, block, x_peer)
            to_y[k] = send(block, block, y_peer)
            to_core[k].append(send(block, block, core_peer))
        k = t - 1
        if 0 <= k < ZS:
            to_x[k].wait_recv()
            block = place(behind(k), 1 - x, y)
            turn_y[k] = send(block.at[upper], block.at[upper], y_peer)
            to_core[k].append(send(block, block, core_peer))
            to_y[k].wait_recv()
            block = place(behind(k), x, 1 - y)
            turn_x[k] = send(block.at[lower], block.at[lower], x_peer)
            to_core[k].append(send(block, block, core_peer))
        k = t - 2
        if 0 <= k < ZS:
            turn_y[k].wait_recv()
            turn_x[k].wait_recv()
            block = place(behind(k), 1 - x, 1 - y)
            to_core[k].append(send(block, block, core_peer))
        k = t - 3
        if 0 <= k < ZS:
            for copy in to_core[k]:
                copy.wait_recv()
            if k == 0:
                loads[1].wait()
                loads[2].wait()

            def feed(xx, unused):
                r = behind(k) * 2 + xx
                wide = flow[r].astype(F32).reshape(tokens, columns)
                square_acc[...] += jnp.sum(wide * wide, axis=1, keepdims=True)
                gained = (wide * (gain_ref[r] * shrink)).astype(BF)
                depth = pl.ds(pl.multiple_of(r * columns, columns), columns)
                gate_acc[...] += jnp.dot(gained, gw[depth, :], preferred_element_type=F32)
                up_acc[...] += jnp.dot(gained, uw[depth, :], preferred_element_type=F32)
                return unused

            lax.fori_loop(0, 2, feed, 0)

    scale = lax.rsqrt(square_acc[...] / (columns * reqs) + epsilon) * (1.0 / shrink)
    gate = gate_acc[...] * scale
    hidden[...] = (gate / (1.0 + jnp.exp(-gate)) * (up_acc[...] * scale)).astype(BF)
    for load in loads[3:]:
        load.wait()

    def ahead(k):
        return lax.rem(z + k, ZS)

    order = list(range(1, ZS)) + [0]
    to_core, turn_y, turn_x, to_x, to_y, along_z = {}, {}, {}, {}, {}, []

    def multiply(j, xx):
        r = ahead(order[j]) * 2 + xx
        term = jnp.dot(hidden[...], dw[r], preferred_element_type=F32)
        term = term.astype(BF).reshape(flow.shape[1], rows, columns)
        for cc in range(2):
            for yy in range(2):
                prod[r, cc, yy] = term[yy * 2 + cc]
        return send(prod.at[r, 1 - c], prod_core.at[r], core_peer)

    def join_core(copy, r):
        copy.wait_recv()
        prod[r, c] = (prod[r, c].astype(F32) + prod_core[r].astype(F32)).astype(BF)

    def far(j):
        to_core[j, 0] = multiply(j, 1 - x)

    def near(j):
        to_core[j, 1] = multiply(j, x)

    def turn(j):
        r = ahead(order[j]) * 2 + 1 - x
        join_core(to_core[j, 0], r)
        block = prod.at[r, c, 1 - y]
        turn_y[j] = send(block.at[upper], diag_y.at[j], y_peer)
        turn_x[j] = send(block.at[lower], diag_x.at[j], x_peer)

    def over_x(j):
        turn_y[j].wait_recv()
        block = prod.at[ahead(order[j]) * 2 + 1 - x, c, y]
        block[upper] = (block[upper].astype(F32) + diag_y[j].astype(F32)).astype(BF)
        to_x[j] = send(block, from_x.at[j], x_peer)

    def over_y(j):
        r = ahead(order[j]) * 2 + x
        join_core(to_core[j, 1], r)
        turn_x[j].wait_recv()
        block = prod.at[r, c, 1 - y]
        block[lower] = (block[lower].astype(F32) + diag_x[j].astype(F32)).astype(BF)
        to_y[j] = send(block, from_y.at[j], y_peer)

    def finish(j):
        to_x[j].wait_recv()
        to_y[j].wait_recv()
        block = prod.at[ahead(order[j]) * 2 + x, c, y]
        total = block[...].astype(F32) + (from_x[j].astype(F32) + from_y[j].astype(F32))
        if order[j] > 0:
            block[...] = total.astype(BF)
            along_z.append(send(block, from_z.at[j], z_peer(order[j])))
        return total

    far(0)
    far(1)
    turn(0)
    near(0)
    turn(1)
    far(2)
    over_x(0)
    over_y(0)
    turn(2)
    near(1)
    over_x(1)
    over_y(1)
    far(3)
    turn(3)
    near(2)
    finish(0)
    over_x(2)
    over_y(2)
    near(3)
    finish(1)
    over_x(3)
    over_y(3)
    finish(2)
    total = finish(3)
    for j, copy in enumerate(along_z):
        copy.wait_recv()
        total = total + from_z[j].astype(F32)
    out_ref[...] = (flow[req, tp].astype(F32) + total).astype(BF)
    for copy in sent:
        copy.wait_send()


def rest(attended, out_weight, residual, norm_gain, gate_weight, up_weight, down_weight, reqs, tps):
    rows, columns = residual.shape
    tokens, depth = attended.shape
    hidden_here = gate_weight.shape[1]
    vmem = pl.BlockSpec(memory_space=pltpu.VMEM)
    anywhere = pl.BlockSpec(memory_space=pl.ANY)
    copies = 2 * ZS + 1 + (ZS - 1) + 8 * ZS + 6 * ZS + (ZS - 1)
    half = rows // 2
    return pl.pallas_call(
        rest_kernel,
        out_shape=jax.ShapeDtypeStruct((rows, columns), BF),
        in_specs=[vmem, anywhere, vmem, vmem, anywhere, anywhere, anywhere],
        out_specs=vmem,
        scratch_shapes=[
            pltpu.VMEM((reqs, tokens, depth), BF),
            pltpu.VMEM(out_weight.shape, BF),
            pltpu.VMEM(gate_weight.shape, BF),
            pltpu.VMEM(up_weight.shape, BF),
            pltpu.VMEM((reqs, hidden_here, columns), BF),
            pltpu.VMEM((2, 2, rows, columns), BF),
            pltpu.VMEM((2, rows, columns), BF),
            pltpu.VMEM((rows, columns), BF),
            pltpu.VMEM((rows, columns), BF),
            pltpu.VMEM((reqs, tps, rows, columns), BF),
            pltpu.VMEM((rows * tps, hidden_here), F32),
            pltpu.VMEM((rows * tps, hidden_here), F32),
            pltpu.VMEM((rows * tps, 1), F32),
            pltpu.VMEM((rows * tps, hidden_here), BF),
            pltpu.VMEM((reqs, 2, 2, rows, columns), BF),
            pltpu.VMEM((reqs, 2, rows, columns), BF),
            pltpu.VMEM((ZS, half, columns), BF),
            pltpu.VMEM((ZS, half, columns), BF),
            pltpu.VMEM((ZS, rows, columns), BF),
            pltpu.VMEM((ZS, rows, columns), BF),
            pltpu.VMEM((ZS - 1, rows, columns), BF),
            pltpu.SemaphoreType.DMA((3 + reqs,)),
            pltpu.SemaphoreType.DMA((copies,)),
            pltpu.SemaphoreType.DMA((copies,)),
        ],
        compiler_params=pltpu.CompilerParams(
            collective_id=0, has_side_effects=True, vmem_limit_bytes=60 * 2**20
        ),
        name="rest",
    )(
        attended, out_weight, residual, norm_gain.reshape(reqs, 1, columns),
        gate_weight, up_weight, down_weight,
    )


def per_device(
    queries, new_keys, new_values, cache_keys, cache_values, tok_req, cache_req,
    out_weight, residual, norm_gain, gate_weight, up_weight, down_weight,
):
    attended = attend(queries, new_keys, new_values, cache_keys, cache_values, tok_req, cache_req)
    reqs, tps = lax.axis_size("req"), lax.axis_size("tp")
    if reqs == 2 * ZS and tps == 4 and residual.shape[0] % 32 == 0 and residual.shape[1] % 128 == 0:
        return rest(
            attended, out_weight, residual, norm_gain, gate_weight, up_weight, down_weight, reqs, tps
        )
    partial_out = jnp.dot(
        lax.all_gather(attended, "req", axis=0, tiled=True),
        out_weight,
        preferred_element_type=F32,
    )
    mixed = lax.psum_scatter(
        partial_out.astype(BF), "tp", scatter_dimension=0, tiled=True
    ).astype(F32)
    stream = (residual.astype(F32) + mixed).astype(BF)
    whole = lax.all_gather(stream, "req", axis=1, tiled=True)
    whole = lax.all_gather(whole, "tp", axis=0, tiled=True).astype(F32)
    mean_square = jnp.mean(whole * whole, axis=1, keepdims=True)
    normed = (whole * lax.rsqrt(mean_square + epsilon) * norm_gain[None, :]).astype(BF)
    gate = jnp.dot(normed, gate_weight, preferred_element_type=F32)
    up = jnp.dot(normed, up_weight, preferred_element_type=F32)
    hidden = (jax.nn.silu(gate) * up).astype(BF)
    product = jnp.dot(hidden, down_weight, preferred_element_type=F32)
    summed = lax.psum_scatter(product, "tp", scatter_dimension=0, tiled=True)
    summed = lax.psum_scatter(summed, "req", scatter_dimension=1, tiled=True)
    return (stream.astype(F32) + summed).astype(BF)


def solution(mesh):
    in_specs = (
        P("req", "tp"),
        P("req", "tp"),
        P("req", "tp"),
        P("req", "tp"),
        P("req", "tp"),
        P("req"),
        P("req"),
        P("tp", "req"),
        P("tp", "req"),
        P(),
        P(None, ("req", "tp")),
        P(None, ("req", "tp")),
        P(("req", "tp"), None),
    )
    out_specs = P("tp", "req")
    return jax.shard_map(
        per_device, mesh=mesh, in_specs=in_specs, out_specs=out_specs, check_vma=False
    )
```

```python
import functools
import math

import jax
import jax.numpy as jnp
from jax import lax
from jax.experimental import pallas as pl
from jax.experimental.pallas import tpu as pltpu
from jax.sharding import PartitionSpec as P

HD = 128
epsilon = 1e-05
masked_value = -1e30
key_block = 1024
score_factor = math.log2(math.e) / math.sqrt(HD)
BF = jnp.bfloat16
F32 = jnp.float32


def attend_kernel(
    first_ref, count_ref, bounds_ref, q_ref, nk_ref, nv_ref, ck_ref, cv_ref, out_ref,
    kbuf, vbuf, ksem, vsem, m_ref, l_ref, acc_ref, wide_q, spread, placed, wide_out,
):
    windows = bounds_ref.shape[0]
    kv = acc_ref.shape[1] // HD
    span = q_ref.shape[0] // windows
    padded = acc_ref.shape[0] // (kv * span)
    group = q_ref.shape[1] // (kv * HD)
    pool = ck_ref.shape[0]
    width = kbuf.shape[1]
    slots = kbuf.shape[0]
    ahead = slots - 1

    def copies(w, b, slot):
        start = jnp.minimum(first_ref[w] + b * width, pool - width)
        start = pl.multiple_of(start, 16)
        rows = pl.ds(start, width)
        return (
            pltpu.make_async_copy(ck_ref.at[rows], kbuf.at[slot], ksem.at[slot]),
            pltpu.make_async_copy(cv_ref.at[rows], vbuf.at[slot], vsem.at[slot]),
        )

    def advance(w, b):
        last = b + 1 >= count_ref[jnp.minimum(w, windows - 1)]
        return jnp.where(last, w + 1, w), jnp.where(last, 0, b + 1)

    def fetch(w, b, slot):
        @pl.when(w < windows)
        def _():
            for c in copies(w, b, slot):
                c.start()

    w0, b0 = jnp.int32(0), jnp.int32(0)
    for i in range(ahead):
        fetch(w0, b0, i)
        w0, b0 = advance(w0, b0)

    wide_q[...] = q_ref[...].astype(F32)
    spread[...] = jnp.zeros_like(spread)
    placed[...] = jnp.zeros_like(placed)
    per_head = span * padded

    def head_rows(g):
        return pl.ds(g, span, stride=padded)

    def own(h):
        return slice(h * per_head, (h + 1) * per_head), slice(h * HD, (h + 1) * HD)

    def scores_of(keys, q, low, high):
        s = lax.dot_general(
            q, keys, (((1,), (1,)), ((), ())), preferred_element_type=F32
        )
        pos = lax.broadcasted_iota(jnp.int32, s.shape, 1)
        return jnp.where((pos >= low) & (pos < high), s * score_factor, masked_value)

    def weigh(p, values):
        return jnp.dot(p, values, preferred_element_type=F32)

    def window(w, carry):
        low, high = bounds_ref[w, :, 0:1], bounds_ref[w, :, 1:2]
        tokens = pl.ds(pl.multiple_of(w * span, span), span)
        for h in range(kv):
            for g in range(group):
                at = (h * group + g) * HD
                spread[h, head_rows(g), :] = wide_q[tokens, at : at + HD]
            placed[own(h)] = spread[h].astype(BF)
        s = scores_of(nk_ref[...], placed[...], bounds_ref[w, :, 2:3], bounds_ref[w, :, 3:4])
        m = jnp.max(s, axis=1, keepdims=True)
        p = jnp.exp2(s - m).astype(BF)
        m_ref[...] = m
        l_ref[...] = jnp.sum(p.astype(F32), axis=1, keepdims=True)
        acc_ref[...] = weigh(p, nv_ref[...])

        def block(b, inner):
            item, wn, bn = inner
            slot = lax.rem(item, slots)
            fetch(wn, bn, lax.rem(item + ahead, slots))
            for c in copies(w, b, slot):
                c.wait()
            nominal = first_ref[w] + b * width
            start = jnp.minimum(nominal, pool - width)
            s = scores_of(kbuf[slot], placed[...], jnp.maximum(low, nominal) - start, high - start)
            m_old = m_ref[...]
            m_new = jnp.maximum(m_old, jnp.max(s, axis=1, keepdims=True))
            alpha = jnp.exp2(m_old - m_new)
            p = jnp.exp2(s - m_new).astype(BF)
            m_ref[...] = m_new
            l_ref[...] = l_ref[...] * alpha + jnp.sum(p.astype(F32), axis=1, keepdims=True)
            acc_ref[...] = acc_ref[...] * alpha + weigh(p, vbuf[slot])
            return (item + 1, *advance(wn, bn))

        carry = lax.fori_loop(0, count_ref[w], block, carry)
        scaled = acc_ref[...] / l_ref[...]
        for h in range(kv):
            spread[h] = scaled[own(h)]
            for g in range(group):
                at = (h * group + g) * HD
                wide_out[tokens, at : at + HD] = spread[h, head_rows(g), :]
        return carry

    lax.fori_loop(0, windows, window, (jnp.int32(0), w0, b0))
    out_ref[...] = wide_out[...].astype(BF)


def attend(queries, new_keys, new_values, cache_keys, cache_values, tok_req, cache_req):
    tokens = queries.shape[0]
    kv = new_keys.shape[1] // HD
    group = queries.shape[1] // (kv * HD)
    padded = (group + 7) // 8 * 8
    span = max(1, min(tokens, 128 // (padded * kv)))
    windows = tokens // span
    columns = kv * span * padded
    depth = kv * HD
    pool = cache_keys.shape[0]
    width = min(key_block, pool)

    owner = jnp.where(cache_req < 0, 2**30, cache_req)[None, :]
    low = jnp.sum((owner < tok_req[:, None]).astype(jnp.int32), axis=1)
    high = jnp.sum((owner <= tok_req[:, None]).astype(jnp.int32), axis=1)
    new_low = jnp.sum((tok_req[None, :] < tok_req[:, None]).astype(jnp.int32), axis=1)
    new_high = jnp.arange(1, tokens + 1, dtype=jnp.int32)
    first = jnp.min(low.reshape(windows, span), axis=1) // 16 * 16
    last = jnp.max(high.reshape(windows, span), axis=1)
    count = jnp.maximum((last - first + width - 1) // width, 1)
    bounds = jnp.stack([low, high, new_low, new_high], axis=1).reshape(windows, 1, span, 1, 4)
    bounds = jnp.broadcast_to(bounds, (windows, kv, span, padded, 4)).reshape(windows, columns, 4)

    vmem = pl.BlockSpec(memory_space=pltpu.VMEM)
    smem = pl.BlockSpec(memory_space=pltpu.SMEM)
    anywhere = pl.BlockSpec(memory_space=pl.ANY)
    slots = 4
    return pl.pallas_call(
        attend_kernel,
        out_shape=jax.ShapeDtypeStruct(queries.shape, BF),
        in_specs=[smem, smem, vmem, vmem, vmem, vmem, anywhere, anywhere],
        out_specs=vmem,
        scratch_shapes=[
            pltpu.VMEM((slots, width, depth), BF),
            pltpu.VMEM((slots, width, depth), BF),
            pltpu.SemaphoreType.DMA((slots,)),
            pltpu.SemaphoreType.DMA((slots,)),
            pltpu.VMEM((columns, 1), F32),
            pltpu.VMEM((columns, 1), F32),
            pltpu.VMEM((columns, depth), F32),
            pltpu.VMEM(queries.shape, F32),
            pltpu.VMEM((kv, span * padded, HD), F32),
            pltpu.VMEM((columns, depth), BF),
            pltpu.VMEM(queries.shape, F32),
        ],
        compiler_params=pltpu.CompilerParams(vmem_limit_bytes=60 * 2**20),
        name="attend",
    )(first, count, bounds, queries, new_keys, new_values, cache_keys, cache_values)


MESH = pl.DeviceIdType.MESH
ZS = 4
shrink = 2.0**-24


def rest_kernel(
    att_ref, ow_hbm, res_ref, gain_ref, gw_hbm, uw_hbm, dw_hbm, out_ref,
    att, ow, gw, uw, dw, part, core_in, y_out, y_in, flow, gate_acc, up_acc, square_acc,
    hidden, prod, prod_core, diag_y, diag_x, from_x, from_y, from_z,
    local, send_sem, recv_sem,
):
    req, tp = lax.axis_index("req"), lax.axis_index("tp")
    z, x, y, c = req // 2, lax.rem(req, 2), tp // 2, lax.rem(tp, 2)
    columns = out_ref.shape[1]
    rows = out_ref.shape[0]
    half = rows // 2
    reqs = flow.shape[0]
    tokens = rows * flow.shape[1]
    upper, lower = pl.ds(0, half), pl.ds(half, half)

    loads = [
        pltpu.make_async_copy(ow_hbm, ow, local.at[0]),
        pltpu.make_async_copy(gw_hbm, gw, local.at[1]),
        pltpu.make_async_copy(uw_hbm, uw, local.at[2]),
    ]
    for r in range(reqs):
        part_cols = pl.ds(r * columns, columns)
        loads.append(pltpu.make_async_copy(dw_hbm.at[:, part_cols], dw.at[r], local.at[3 + r]))
    for load in loads:
        load.start()

    core_peer = (req, y * 2 + 1 - c)
    y_peer = (req, (1 - y) * 2 + c)
    x_peer = (z * 2 + 1 - x, tp)

    def z_peer(k):
        return (lax.rem(z + k, ZS) * 2 + x, tp)

    barrier = pltpu.get_barrier_semaphore()
    peers = [core_peer, y_peer, x_peer] + [z_peer(k) for k in range(1, ZS)]
    for peer in peers:
        pl.semaphore_signal(barrier, inc=1, device_id=peer, device_id_type=MESH)
    pl.semaphore_wait(barrier, len(peers))

    sent = []

    def send(src, dst, peer):
        i = len(sent)
        copy = pltpu.make_async_remote_copy(
            src_ref=src, dst_ref=dst, send_sem=send_sem.at[i], recv_sem=recv_sem.at[i],
            device_id=peer, device_id_type=MESH,
        )
        copy.start()
        sent.append(copy)
        return copy

    def behind(k):
        return lax.rem(z - k + ZS, ZS)

    along_z = [None] + [send(att_ref, att.at[req], z_peer(k)) for k in range(1, ZS)]
    across = [send(att_ref, att.at[req], x_peer)]
    att[req] = att_ref[...]
    for k in range(1, ZS):
        along_z[k].wait_recv()
        block = att.at[behind(k) * 2 + x]
        across.append(send(block, block, x_peer))
    for copy in across:
        copy.wait_recv()
    loads[0].wait()
    mixed = jnp.dot(
        att[...].reshape(tokens, att.shape[2]), ow[...], preferred_element_type=F32
    ).astype(BF).reshape(flow.shape[1], rows, columns)
    for cc in range(2):
        for yy in range(2):
            part[cc, yy] = mixed[yy * 2 + cc]
    copy = send(part.at[1 - c], core_in, core_peer)
    copy.wait_recv()
    y_out[...] = (part[c, 1 - y].astype(F32) + core_in[1 - y].astype(F32)).astype(BF)
    copy = send(y_out, y_in, y_peer)
    kept = part[c, y].astype(F32) + core_in[y].astype(F32)
    copy.wait_recv()
    stream = (res_ref[...].astype(F32) + (kept + y_in[...].astype(F32))).astype(BF)
    flow[req, tp] = stream

    def place(zz, xx, yy):
        return flow.at[zz * 2 + xx, yy * 2 + c]

    own = flow.at[req, tp]
    along_z = [None] + [send(own, own, z_peer(k)) for k in range(1, ZS)]
    to_x, to_y, turn_y, turn_x = {}, {}, {}, {}
    to_core = {k: [] for k in range(ZS)}
    gate_acc[...] = jnp.zeros_like(gate_acc)
    up_acc[...] = jnp.zeros_like(up_acc)
    square_acc[...] = jnp.zeros_like(square_acc)
    for t in range(ZS + 3):
        k = t
        if k < ZS:
            if k > 0:
                along_z[k].wait_recv()
            block = place(behind(k), x, y)
            to_x[k] = send(block, block, x_peer)
            to_y[k] = send(block, block, y_peer)
            to_core[k].append(send(block, block, core_peer))
        k = t - 1
        if 0 <= k < ZS:
            to_x[k].wait_recv()
            block = place(behind(k), 1 - x, y)
            turn_y[k] = send(block.at[upper], block.at[upper], y_peer)
            to_core[k].append(send(block, block, core_peer))
            to_y[k].wait_recv()
            block = place(behind(k), x, 1 - y)
            turn_x[k] = send(block.at[lower], block.at[lower], x_peer)
            to_core[k].append(send(block, block, core_peer))
        k = t - 2
        if 0 <= k < ZS:
            turn_y[k].wait_recv()
            turn_x[k].wait_recv()
            block = place(behind(k), 1 - x, 1 - y)
            to_core[k].append(send(block, block, core_peer))
        k = t - 3
        if 0 <= k < ZS:
            for copy in to_core[k]:
                copy.wait_recv()
            if k == 0:
                loads[1].wait()
                loads[2].wait()

            def feed(xx, unused):
                r = behind(k) * 2 + xx
                wide = flow[r].astype(F32).reshape(tokens, columns)
                square_acc[...] += jnp.sum(wide * wide, axis=1, keepdims=True)
                gained = (wide * (gain_ref[r] * shrink)).astype(BF)
                depth = pl.ds(pl.multiple_of(r * columns, columns), columns)
                gate_acc[...] += jnp.dot(gained, gw[depth, :], preferred_element_type=F32)
                up_acc[...] += jnp.dot(gained, uw[depth, :], preferred_element_type=F32)
                return unused

            lax.fori_loop(0, 2, feed, 0)

    scale = lax.rsqrt(square_acc[...] / (columns * reqs) + epsilon) * (1.0 / shrink)
    gate = gate_acc[...] * scale
    hidden[...] = (gate / (1.0 + jnp.exp(-gate)) * (up_acc[...] * scale)).astype(BF)
    for load in loads[3:]:
        load.wait()

    def ahead(k):
        return lax.rem(z + k, ZS)

    order = list(range(1, ZS)) + [0]
    to_core, turn_y, turn_x, to_x, to_y, along_z = {}, {}, {}, {}, {}, []

    def multiply(j, xx):
        r = ahead(order[j]) * 2 + xx
        term = jnp.dot(hidden[...], dw[r], preferred_element_type=F32)
        term = term.astype(BF).reshape(flow.shape[1], rows, columns)
        for cc in range(2):
            for yy in range(2):
                prod[r, cc, yy] = term[yy * 2 + cc]
        return send(prod.at[r, 1 - c], prod_core.at[r], core_peer)

    def join_core(copy, r):
        copy.wait_recv()
        prod[r, c] = (prod[r, c].astype(F32) + prod_core[r].astype(F32)).astype(BF)

    def far(j):
        to_core[j, 0] = multiply(j, 1 - x)

    def near(j):
        to_core[j, 1] = multiply(j, x)

    def turn(j):
        r = ahead(order[j]) * 2 + 1 - x
        join_core(to_core[j, 0], r)
        block = prod.at[r, c, 1 - y]
        turn_y[j] = send(block.at[upper], diag_y.at[j], y_peer)
        turn_x[j] = send(block.at[lower], diag_x.at[j], x_peer)

    def over_x(j):
        turn_y[j].wait_recv()
        block = prod.at[ahead(order[j]) * 2 + 1 - x, c, y]
        block[upper] = (block[upper].astype(F32) + diag_y[j].astype(F32)).astype(BF)
        to_x[j] = send(block, from_x.at[j], x_peer)

    def over_y(j):
        r = ahead(order[j]) * 2 + x
        join_core(to_core[j, 1], r)
        turn_x[j].wait_recv()
        block = prod.at[r, c, 1 - y]
        block[lower] = (block[lower].astype(F32) + diag_x[j].astype(F32)).astype(BF)
        to_y[j] = send(block, from_y.at[j], y_peer)

    def finish(j):
        to_x[j].wait_recv()
        to_y[j].wait_recv()
        block = prod.at[ahead(order[j]) * 2 + x, c, y]
        total = block[...].astype(F32) + (from_x[j].astype(F32) + from_y[j].astype(F32))
        if order[j] > 0:
            block[...] = total.astype(BF)
            along_z.append(send(block, from_z.at[j], z_peer(order[j])))
        return total

    far(0)
    far(1)
    turn(0)
    near(0)
    turn(1)
    far(2)
    over_x(0)
    over_y(0)
    turn(2)
    near(1)
    over_x(1)
    over_y(1)
    far(3)
    turn(3)
    near(2)
    finish(0)
    over_x(2)
    over_y(2)
    near(3)
    finish(1)
    over_x(3)
    over_y(3)
    finish(2)
    total = finish(3)
    for j, copy in enumerate(along_z):
        copy.wait_recv()
        total = total + from_z[j].astype(F32)
    out_ref[...] = (flow[req, tp].astype(F32) + total).astype(BF)
    for copy in sent:
        copy.wait_send()


def rest(attended, out_weight, residual, norm_gain, gate_weight, up_weight, down_weight, reqs, tps):
    rows, columns = residual.shape
    tokens, depth = attended.shape
    hidden_here = gate_weight.shape[1]
    vmem = pl.BlockSpec(memory_space=pltpu.VMEM)
    anywhere = pl.BlockSpec(memory_space=pl.ANY)
    copies = 2 * ZS + 1 + (ZS - 1) + 8 * ZS + 6 * ZS + (ZS - 1)
    half = rows // 2
    return pl.pallas_call(
        rest_kernel,
        out_shape=jax.ShapeDtypeStruct((rows, columns), BF),
        in_specs=[vmem, anywhere, vmem, vmem, anywhere, anywhere, anywhere],
        out_specs=vmem,
        scratch_shapes=[
            pltpu.VMEM((reqs, tokens, depth), BF),
            pltpu.VMEM(out_weight.shape, BF),
            pltpu.VMEM(gate_weight.shape, BF),
            pltpu.VMEM(up_weight.shape, BF),
            pltpu.VMEM((reqs, hidden_here, columns), BF),
            pltpu.VMEM((2, 2, rows, columns), BF),
            pltpu.VMEM((2, rows, columns), BF),
            pltpu.VMEM((rows, columns), BF),
            pltpu.VMEM((rows, columns), BF),
            pltpu.VMEM((reqs, tps, rows, columns), BF),
            pltpu.VMEM((rows * tps, hidden_here), F32),
            pltpu.VMEM((rows * tps, hidden_here), F32),
            pltpu.VMEM((rows * tps, 1), F32),
            pltpu.VMEM((rows * tps, hidden_here), BF),
            pltpu.VMEM((reqs, 2, 2, rows, columns), BF),
            pltpu.VMEM((reqs, 2, rows, columns), BF),
            pltpu.VMEM((ZS, half, columns), BF),
            pltpu.VMEM((ZS, half, columns), BF),
            pltpu.VMEM((ZS, rows, columns), BF),
            pltpu.VMEM((ZS, rows, columns), BF),
            pltpu.VMEM((ZS - 1, rows, columns), BF),
            pltpu.SemaphoreType.DMA((3 + reqs,)),
            pltpu.SemaphoreType.DMA((copies,)),
            pltpu.SemaphoreType.DMA((copies,)),
        ],
        compiler_params=pltpu.CompilerParams(
            collective_id=0, has_side_effects=True, vmem_limit_bytes=60 * 2**20
        ),
        name="rest",
    )(
        attended, out_weight, residual, norm_gain.reshape(reqs, 1, columns),
        gate_weight, up_weight, down_weight,
    )


def per_device(
    queries, new_keys, new_values, cache_keys, cache_values, tok_req, cache_req,
    out_weight, residual, norm_gain, gate_weight, up_weight, down_weight,
):
    attended = attend(queries, new_keys, new_values, cache_keys, cache_values, tok_req, cache_req)
    reqs, tps = lax.axis_size("req"), lax.axis_size("tp")
    if reqs == 2 * ZS and tps == 4 and residual.shape[0] % 32 == 0 and residual.shape[1] % 128 == 0:
        return rest(
            attended, out_weight, residual, norm_gain, gate_weight, up_weight, down_weight, reqs, tps
        )
    partial_out = jnp.dot(
        lax.all_gather(attended, "req", axis=0, tiled=True),
        out_weight,
        preferred_element_type=F32,
    )
    mixed = lax.psum_scatter(
        partial_out.astype(BF), "tp", scatter_dimension=0, tiled=True
    ).astype(F32)
    stream = (residual.astype(F32) + mixed).astype(BF)
    whole = lax.all_gather(stream, "req", axis=1, tiled=True)
    whole = lax.all_gather(whole, "tp", axis=0, tiled=True).astype(F32)
    mean_square = jnp.mean(whole * whole, axis=1, keepdims=True)
    normed = (whole * lax.rsqrt(mean_square + epsilon) * norm_gain[None, :]).astype(BF)
    gate = jnp.dot(normed, gate_weight, preferred_element_type=F32)
    up = jnp.dot(normed, up_weight, preferred_element_type=F32)
    hidden = (jax.nn.silu(gate) * up).astype(BF)
    product = jnp.dot(hidden, down_weight, preferred_element_type=F32)
    summed = lax.psum_scatter(product, "tp", scatter_dimension=0, tiled=True)
    summed = lax.psum_scatter(summed, "req", scatter_dimension=1, tiled=True)
    return (stream.astype(F32) + summed).astype(BF)


def solution(mesh):
    in_specs = (
        P("req", "tp"),
        P("req", "tp"),
        P("req", "tp"),
        P("req", "tp"),
        P("req", "tp"),
        P("req"),
        P("req"),
        P("tp", "req"),
        P("tp", "req"),
        P(),
        P(None, ("req", "tp")),
        P(None, ("req", "tp")),
        P(("req", "tp"), None),
    )
    out_specs = P("tp", "req")
    return jax.shard_map(
        per_device, mesh=mesh, in_specs=in_specs, out_specs=out_specs, check_vma=False
    )
```
